512 devices in a mesh: seq: 16 (over y, core), hid: 32 (over z, x).
Axes of the slice: x: 4, y: 8, z: 8, core: 2. Of those that a mesh axis runs over, the one named last changes fastest.
Arguments:
- query_stream: bfloat16 [12288, 8192], P('seq', 'hid'), may hold values from -6 to 6
- key_stream: bfloat16 [12288, 8192], P('seq', 'hid'), may hold values from -6 to 6
- value_stream: bfloat16 [12288, 8192], P('seq', 'hid'), may hold values from -6 to 6
- earlier_rows: bfloat16 [127, 8192], P(None, 'hid'), may hold values from -6 to 6
- filter_taps: float32 [8192, 128], P('hid'), may hold values from -0.4 to 0.4
- skip_gain: float32 [8192], P('hid'), may hold values from 0.5 to 1.5
- weight_values: bfloat16 [8192, 8192], P('seq', 'hid'), may hold values from -0.0625 to 0.0625
- weight_scales: float32 [64, 64], P('seq', 'hid'), may hold values from 0.5 to 2
Outputs:
- mixed_out: bfloat16 [12288, 8192], P('seq', 'hid')
The draws below stay inside these ranges and needn't reach their ends.
All inputs are finite; a program needn't handle non-finite values.
Results may differ from the reference program's by a relative error of at most 0.0064.
Values may be sent and summed in bfloat16 or wider, within the bound.
A program may use at most 64 MiB of HBM per device.

```python
import math
import jax
import jax.numpy as jnp
from jax import lax

D = 8192
TAPS = 128
BLOCK = 128
TOKENS = 12288


def draw_filter_taps(key, part):
    key = jax.random.fold_in(key, 11)
    rate_key, tap_key = jax.random.split(key)
    floor_rate, ceil_rate = (0.3, 25.0)
    raw_taps = jnp.clip(jax.random.normal(tap_key, (D, TAPS), jnp.float32), -4.0, 4.0)
    fraction = jax.random.uniform(rate_key, (D, 1), jnp.float32)
    decay_rate = jnp.exp(math.log(floor_rate) + fraction * (math.log(ceil_rate) - math.log(floor_rate))) / TAPS
    lag_index = jnp.arange(TAPS, dtype=jnp.float32)[None, :]
    return 0.1 * raw_taps * jnp.exp(-decay_rate * lag_index)


def levels(rng, shape, pieces, smallest, largest):
    loudness, own = 1.0, jax.random.fold_in(rng, 6)
    for position, blocks in pieces:
        heights = jnp.exp(jax.random.uniform(jax.random.fold_in(own, position), (blocks,), jnp.float32, smallest / len(pieces), largest / len(pieces)))
        loudness = loudness * jnp.repeat(heights, shape[position] // blocks).reshape([-1 if axis == position else 1 for axis in range(len(shape))])
    return loudness


def noise(own_key, extent, scale, limit, cuts=(), kind=jnp.bfloat16):
    loudness = levels(own_key, extent, cuts, -0.22, 0.18) if cuts else 1.0
    values = jax.random.normal(own_key, extent, jnp.float32) * scale * loudness
    return jnp.minimum(jnp.maximum(values, -limit), limit).astype(kind)


def setup_inputs(seed: int = 0) -> dict:
    seeds = jax.random.split(jax.random.key(seed), 9)
    return {
        "query_stream": noise(seeds[0], (TOKENS, D), 1.0, 6.0, ((0, 16), (1, 32))),
        "key_stream": noise(seeds[1], (TOKENS, D), 1.0, 6.0, ((0, 16), (1, 32))),
        "value_stream": noise(seeds[2], (TOKENS, D), 1.0, 6.0, ((0, 16), (1, 32))),
        "earlier_rows": noise(seeds[3], (TAPS - 1, D), 1.0, 6.0, ((1, 32),)),
        "filter_taps": draw_filter_taps(jax.random.fold_in(seeds[8], 71), 0),
        "skip_gain": jnp.clip(0.5 + 1.0 * jax.random.uniform(seeds[5], (D,), jnp.float32) ** levels(seeds[5], (D,), ((0, 32),), -0.2, 0.2), 0.5, 1.5),
        "weight_values": noise(seeds[6], (D, D), D ** -0.5, 0.0625, ((0, 16), (1, 32))),
        "weight_scales": jnp.clip(jnp.exp(math.log(2.0) - 1.3862944 * jax.random.uniform(seeds[7], (D // BLOCK, D // BLOCK), jnp.float32) ** levels(seeds[7], (D // BLOCK, D // BLOCK), ((0, 16), (1, 32)), -0.2, 0.2)), 0.5, 2.0),
    }


def causal_filter(signal, filter_taps):
    width = filter_taps.shape[1]
    count = signal.shape[0] - (width - 1)

    def add_tap(offset, carried):
        shifted = lax.dynamic_slice_in_dim(signal, (width - 1 - offset).astype(jnp.int32), count, 0)
        tap_column = lax.dynamic_slice_in_dim(filter_taps, offset.astype(jnp.int32), 1, 1)[:, 0]
        return carried + shifted * tap_column[None, :]

    start_sum = jnp.zeros((count, signal.shape[1]), jnp.float32)
    return lax.fori_loop(jnp.int32(0), jnp.int32(width), add_tap, start_sum)


def reference(query_stream, key_stream, value_stream, earlier_rows, filter_taps, skip_gain, weight_values, weight_scales):
    product = (key_stream.astype(jnp.float32) * value_stream.astype(jnp.float32)).astype(jnp.bfloat16)
    extended = jnp.concatenate([earlier_rows, product], axis=0).astype(jnp.float32)
    filtered = causal_filter(extended, filter_taps) + skip_gain[None, :] * product.astype(jnp.float32)
    gated = (query_stream.astype(jnp.float32) * filtered).astype(jnp.bfloat16)
    spread = jnp.repeat(jnp.repeat(weight_scales, BLOCK, axis=0), BLOCK, axis=1)
    dequantized = (weight_values.astype(jnp.float32) * spread).astype(jnp.bfloat16)
    total = jnp.dot(gated, dequantized, preferred_element_type=jnp.float32)
    return total.astype(jnp.bfloat16)
```

```python
import functools

import jax
import jax.numpy as jnp
from jax import lax
from jax.experimental import pallas as pl
from jax.experimental.pallas import tpu as pltpu
from jax.sharding import PartitionSpec as P

MESH = pl.DeviceIdType.MESH
X = 4
CORES = 2
BLOCK = 128
LANES = 128
SUB = 8
ROWS = 128


def hops(n, even):
    far = n // 2
    return (far, n - 1 - far) if even else (n - 1 - far, far)


def kernel(
    ny,
    nz,
    q_hbm,
    k_hbm,
    v_hbm,
    e_hbm,
    t_hbm,
    g_hbm,
    w_hbm,
    s_ref,
    o_hbm,
    q_v,
    k_v,
    v_v,
    e_v,
    t_v,
    g_v,
    w_v,
    halo_out,
    halo_in,
    ext,
    taps,
    deq,
    a_buf,
    b_buf,
    c_send,
    c_recv,
    own,
    o_v,
    in_sem,
    halo_sem,
    a_send_sem,
    a_recv_sem,
    b_send_sem,
    b_recv_sem,
    m_send_sem,
    m_recv_sem,
    t_send_sem,
    t_recv_sem,
    c_send_sem,
    c_recv_sem,
    o_sem,
):
    tokens, width = q_v.shape
    chunks = tokens // ROWS
    half = ROWS
    s, hid = lax.axis_index("seq"), lax.axis_index("hid")
    y, c = s // CORES, s % CORES
    z, x = hid // X, hid % X

    def at(y_, c_, z_, x_):
        return (y_ * CORES + c_, z_ * X + x_)

    z_up, z_down = at(y, c, (z + 1) % nz, x), at(y, c, (z + nz - 1) % nz, x)
    y_up, y_down = at((y + 1) % ny, c, z, x), at((y + ny - 1) % ny, c, z, x)
    sibling = at(y, 1 - c, z, x)
    seq_next = ((s + 1) % (ny * CORES), hid)

    loads = [
        pltpu.make_async_copy(src, dst, in_sem.at[n])
        for n, (src, dst) in enumerate(
            (
                (w_hbm, w_v),
                (k_hbm, k_v),
                (v_hbm, v_v),
                (t_hbm, t_v),
                (g_hbm, g_v),
                (q_hbm, q_v),
                (e_hbm, e_v),
            )
        )
    ]
    for load in loads:
        load.start()

    barrier = pltpu.get_barrier_semaphore()
    partners = [
        at(y, (c + dc) % CORES, z, (x + dx) % X)
        for dc in range(CORES)
        for dx in range(X)
        if (dc, dx) != (0, 0)
    ]
    partners += [z_up, z_down, y_up, y_down]
    partners += [at((y + ny + 2 * c - 1) % ny, 1 - c, z, x)]
    for partner in partners:
        pl.semaphore_signal(barrier, inc=1, device_id=partner, device_id_type=MESH)

    loads[0].wait()
    for i in range(w_v.shape[0] // BLOCK):
        for n in range(width // BLOCK):
            rows, cols = pl.ds(i * BLOCK, BLOCK), pl.ds(n * BLOCK, BLOCK)
            deq[rows, cols] = (
                w_v[rows, cols].astype(jnp.float32) * s_ref[i, n]
            ).astype(jnp.bfloat16)

    loads[1].wait()
    loads[2].wait()
    for i in range(chunks):
        rows = pl.ds(i * ROWS, ROWS)
        product = (
            k_v[rows, :].astype(jnp.float32) * v_v[rows, :].astype(jnp.float32)
        ).astype(jnp.bfloat16)
        if i == chunks - 1:
            halo_out[...] = product
        wide = product.astype(jnp.float32)
        for n in range(width // LANES):
            ext[n, pl.ds(ROWS + i * ROWS, ROWS), :] = wide[:, n * LANES : (n + 1) * LANES]

    pl.semaphore_wait(barrier, len(partners))

    def turn(e, core):
        here = (x == 2 * c + e) & (c == core)
        src = deq.at[pl.ds((2 * e + core) * half, half), :]
        dst = b_buf.at[x, pl.ds(pl.multiple_of((2 * y + core) * half, half), half), :]
        remote = pltpu.make_async_remote_copy(
            src_ref=src,
            dst_ref=dst,
            send_sem=t_send_sem.at[e, core],
            recv_sem=t_recv_sem.at[x],
            device_id=at(y, core, z, 2 * c + e),
            device_id_type=MESH,
        )
        local = pltpu.make_async_copy(src, dst, t_recv_sem.at[x])
        return here, remote, local

    turns = [turn(e, core) for e in range(2) for core in range(CORES)]
    for here, remote, local in turns:
        pl.when(jnp.logical_not(here))(remote.start)
        pl.when(here)(local.start)

    halo = pltpu.make_async_remote_copy(
        src_ref=halo_out,
        dst_ref=halo_in,
        send_sem=halo_sem.at[0],
        recv_sem=halo_sem.at[1],
        device_id=seq_next,
        device_id_type=MESH,
    )
    halo.start()

    loads[3].wait()
    loads[4].wait()
    for n in range(width // LANES):
        flat = t_v[n * LANES : (n + 1) * LANES, :].T
        taps[n] = jnp.broadcast_to(flat[:, None, :], taps.shape[1:])
        taps[n, 0] = taps[n, 0] + g_v[:, n * LANES : (n + 1) * LANES]

    loads[5].wait()

    order = [(i + 1) % chunks for i in range(chunks)]

    def preceding():
        loads[6].wait()
        halo.wait_recv()

        @pl.when(s == 0)
        def _():
            early = e_v[...].astype(jnp.float32)
            for n in range(width // LANES):
                ext[n, pl.ds(1, ROWS - 1), :] = early[:, n * LANES : (n + 1) * LANES]

        @pl.when(s != 0)
        def _():
            early = halo_in[...].astype(jnp.float32)
            for n in range(width // LANES):
                ext[n, pl.ds(0, ROWS), :] = early[:, n * LANES : (n + 1) * LANES]

    def filter_chunk(i):
        base = order[i] * ROWS
        tiles = ROWS // SUB
        reach = taps.shape[1] // SUB
        for n in range(width // LANES):

            def phase(b, sums):
                sums = list(sums)
                factor = [taps[n, a * SUB + b] for a in range(reach)]
                for d in range(1 - reach, tiles):
                    value = ext[n, pl.ds(ROWS + base + d * SUB - b, SUB), :]
                    for a in range(reach):
                        if 0 <= d + a < tiles:
                            sums[d + a] = sums[d + a] + factor[a] * value
                return tuple(sums)

            zero = jnp.zeros((SUB, LANES), jnp.float32)
            sums = lax.fori_loop(0, SUB, phase, (zero,) * tiles)
            filtered = jnp.concatenate(sums, axis=0)
            cols = pl.ds(n * LANES, LANES)
            a_buf[z, pl.ds(base, ROWS), cols] = (
                q_v[pl.ds(base, ROWS), cols].astype(jnp.float32) * filtered
            ).astype(jnp.bfloat16)

    def a_copy(i, way, hop):
        step = 1 if way == 0 else -1
        block = a_buf.at[(z + nz - step * hop) % nz, pl.ds(order[i] * ROWS, ROWS), :]
        return pltpu.make_async_remote_copy(
            src_ref=block,
            dst_ref=block,
            send_sem=a_send_sem,
            recv_sem=a_recv_sem.at[i, way, hop],
            device_id=z_up if way == 0 else z_down,
            device_id_type=MESH,
        )

    def a_arrived(i, way, hop):
        step = 1 if way == 0 else -1
        block = a_buf.at[
            (z + nz - step * (hop + 1)) % nz, pl.ds(order[i] * ROWS, ROWS), :
        ]
        pltpu.make_async_copy(block, block, a_recv_sem.at[i, way, hop]).wait()

    def a_forward(i, way, hop):
        a_arrived(i, way, hop)
        if hop + 1 < hops(nz, i % 2 == 0)[way]:
            a_copy(i, way, hop + 1).start()

    def piece_column(p):
        return (x + (2, 1, 3, 0)[p]) % X

    def b_block(p, owner, core):
        rows = pl.ds(pl.multiple_of((2 * owner + core) * half, half), half)
        return b_buf.at[piece_column(p), rows, :]

    def b_copy(p, way, hop):
        step = 1 if way == 0 else -1
        block = b_block(p, (y + ny - step * hop) % ny, c)
        return pltpu.make_async_remote_copy(
            src_ref=block,
            dst_ref=block,
            send_sem=b_send_sem,
            recv_sem=b_recv_sem.at[p, way, hop],
            device_id=y_up if way == 0 else y_down,
            device_id_type=MESH,
        )

    def to_sibling(p, owner):
        block = b_block(p, owner, c)
        pltpu.make_async_remote_copy(
            src_ref=block,
            dst_ref=block,
            send_sem=m_send_sem,
            recv_sem=m_recv_sem.at[p, owner],
            device_id=sibling,
            device_id_type=MESH,
        ).start()

    def b_start(p):
        column = piece_column(p)
        block = b_block(p, y, c)
        pltpu.make_async_copy(block, block, t_recv_sem.at[column]).wait()
        for way in range(2):
            if hops(ny, p % 2 == 0)[way]:
                b_copy(p, way, 0).start()
        to_sibling(p, y)

    def b_forward(p, way, hop):
        step = 1 if way == 0 else -1
        owner = (y + ny - step * (hop + 1)) % ny
        block = b_block(p, owner, c)
        pltpu.make_async_copy(block, block, b_recv_sem.at[p, way, hop]).wait()
        if hop + 1 < hops(ny, p % 2 == 0)[way]:
            b_copy(p, way, hop + 1).start()
        to_sibling(p, owner)

    def b_whole(p):
        for owner in range(ny):
            block = b_block(p, owner, 1 - c)
            pltpu.make_async_copy(block, block, m_recv_sem.at[p, owner]).wait()

    def multiply(i, p):
        rows = pl.ds(order[i] * ROWS, ROWS)
        left = jnp.concatenate([a_buf[k, rows, :] for k in range(nz)], axis=1)
        total = jnp.dot(
            left, b_buf[piece_column(p)], preferred_element_type=jnp.float32
        )
        if p == X - 1:
            own[rows, :] = total
            return
        c_send[p, rows, :] = total.astype(jnp.bfloat16)
        pltpu.make_async_remote_copy(
            src_ref=c_send.at[p, rows, :],
            dst_ref=c_recv.at[p, rows, :],
            send_sem=c_send_sem,
            recv_sem=c_recv_sem.at[i, p],
            device_id=at(y, c, z, piece_column(p)),
            device_id_type=MESH,
        ).start()

    def finish(i):
        rows = pl.ds(order[i] * ROWS, ROWS)
        total = own[rows, :]
        for p in range(X - 1):
            block = c_recv.at[p, rows, :]
            pltpu.make_async_copy(block, block, c_recv_sem.at[i, p]).wait()
            total = total + c_recv[p, rows, :].astype(jnp.float32)
        o_v[rows, :] = total.astype(jnp.bfloat16)
        pltpu.make_async_copy(o_v.at[rows, :], o_hbm.at[rows, :], o_sem).start()

    far_a, far_b = nz // 2, ny // 2
    last = max(chunks + far_a, X + far_b)
    todo = []
    ready = []
    for k in range(last):
        if k < chunks:
            if order[k] == 0:
                preceding()
            filter_chunk(k)
            for way in range(2):
                if hops(nz, k % 2 == 0)[way]:
                    a_copy(k, way, 0).start()
        if k < X:
            b_start(k)
        events = []
        for hop in reversed(range(max(far_a, far_b))):
            for way in range(2):
                i = k - 1 - hop
                if 0 <= i < chunks and hop < hops(nz, i % 2 == 0)[way]:
                    events.append(functools.partial(a_forward, i, way, hop))
                if 0 <= i < X and hop < hops(ny, i % 2 == 0)[way]:
                    events.append(functools.partial(b_forward, i, way, hop))
        share = -(-len(todo) // max(1, len(events)))
        for event in events:
            event()
            for work in todo[:share]:
                work()
            del todo[:share]
        for work in todo:
            work()
        todo = []
        p = k - far_b
        if 0 <= p < X:
            todo.append(functools.partial(b_whole, p))
            todo += [
                functools.partial(multiply, i, p)
                for i in range(min(chunks, max(0, k - far_a)))
            ]
        i = k - far_a
        if 0 <= i < chunks:
            todo += [
                functools.partial(multiply, i, p)
                for p in range(min(X, k - far_b + 1))
            ]
        for i in ready:
            todo.append(functools.partial(finish, i))
        ready = []
        if k - far_b >= X - 1:
            done = min(chunks, k - far_a + 1)
            first = 0 if k - far_b == X - 1 else max(0, k - far_a)
            ready = list(range(first, done))
    for work in todo:
        work()
    for i in ready:
        finish(i)

    for here, remote, local in turns:
        pl.when(jnp.logical_not(here))(remote.wait_send)
    halo.wait_send()
    sent = a_buf.at[pl.ds(0, nz - 1)]
    pltpu.make_async_copy(sent, sent, a_send_sem).wait()
    sent = b_buf.at[:, pl.ds(0, (ny - 1) * half), :]
    pltpu.make_async_copy(sent, sent, b_send_sem).wait()
    sent = b_buf.at[:, pl.ds(0, ny * half), :]
    pltpu.make_async_copy(sent, sent, m_send_sem).wait()
    pltpu.make_async_copy(c_send, c_send, c_send_sem).wait()
    pltpu.make_async_copy(o_v, o_v, o_sem).wait()


def on_device(ny, nz, q, k, v, earlier, taps, gain, weight, scales):
    tokens, width = q.shape
    depth = weight.shape[0]
    reach = taps.shape[1]
    chunks = tokens // ROWS
    vmem, dma = pltpu.VMEM, pltpu.SemaphoreType.DMA
    bf16, f32 = jnp.bfloat16, jnp.float32
    anywhere = pl.BlockSpec(memory_space=pl.ANY)
    gain = gain.reshape(1, width)
    return pl.pallas_call(
        functools.partial(kernel, ny, nz),
        out_shape=jax.ShapeDtypeStruct((tokens, width), bf16),
        in_specs=[anywhere] * 7 + [pl.BlockSpec(memory_space=pltpu.SMEM)],
        out_specs=anywhere,
        scratch_shapes=[
            vmem(q.shape, bf16),
            vmem(k.shape, bf16),
            vmem(v.shape, bf16),
            vmem(earlier.shape, bf16),
            vmem(taps.shape, f32),
            vmem(gain.shape, f32),
            vmem(weight.shape, bf16),
            vmem((ROWS, width), bf16),
            vmem((ROWS, width), bf16),
            vmem((width // LANES, ROWS + tokens, LANES), f32),
            vmem((width // LANES, reach, SUB, LANES), f32),
            vmem((depth, width), bf16),
            vmem((nz, tokens, width), bf16),
            vmem((X, nz * width, width), bf16),
            vmem((X - 1, tokens, width), bf16),
            vmem((X - 1, tokens, width), bf16),
            vmem((tokens, width), f32),
            vmem((tokens, width), bf16),
            dma((7,)),
            dma((2,)),
            dma,
            dma((chunks, 2, nz // 2)),
            dma,
            dma((X, 2, ny // 2)),
            dma,
            dma((X, ny)),
            dma((2, CORES)),
            dma((X,)),
            dma,
            dma((chunks, X - 1)),
            dma,
        ],
        compiler_params=pltpu.CompilerParams(
            collective_id=0, has_side_effects=True, vmem_limit_bytes=40 * 1024 * 1024
        ),
        cost_estimate=pl.CostEstimate(
            flops=2 * tokens * nz * width * X * width,
            bytes_accessed=4 * tokens * width * 2,
            transcendentals=0,
        ),
    )(q, k, v, earlier, taps, gain, weight, scales)


def solution(mesh):
    ny = mesh.shape["seq"] // CORES
    nz = mesh.shape["hid"] // X
    return jax.shard_map(
        functools.partial(on_device, ny, nz),
        mesh=mesh,
        in_specs=(
            P("seq", "hid"),
            P("seq", "hid"),
            P("seq", "hid"),
            P(None, "hid"),
            P("hid", None),
            P("hid"),
            P("seq", "hid"),
            P("seq", "hid"),
        ),
        out_specs=P("seq", "hid"),
        check_vma=False,
    )
```

```python
import functools

import jax
import jax.numpy as jnp
from jax import lax
from jax.experimental import pallas as pl
from jax.experimental.pallas import tpu as pltpu
from jax.sharding import PartitionSpec as P

MESH = pl.DeviceIdType.MESH
X = 4
CORES = 2
BLOCK = 128
LANES = 128
SUB = 8
ROWS = 128
FILTER, A_BEGIN, A_FORWARD, B_BEGIN, B_FORWARD, B_WHOLE, MULTIPLY, FINISH = range(8)
PLAN = (
    (A_BEGIN, 0), (FILTER, 1), (B_BEGIN, 0), (A_BEGIN, 1), (FILTER, 2), (B_BEGIN, 1), (A_BEGIN, 2), (FILTER, 3),
    (A_FORWARD, 0, 0, 0), (A_FORWARD, 0, 1, 0), (B_BEGIN, 2), (B_FORWARD, 0, 0, 0), (A_FORWARD, 1, 0, 0),
    (A_FORWARD, 1, 1, 0), (B_FORWARD, 0, 1, 0), (FILTER, 4), (B_FORWARD, 1, 0, 0), (A_FORWARD, 2, 0, 0),
    (A_FORWARD, 2, 1, 0), (B_FORWARD, 1, 1, 0), (FILTER, 5), (A_FORWARD, 0, 0, 1), (A_FORWARD, 0, 1, 1),
    (B_FORWARD, 2, 0, 0), (B_FORWARD, 2, 1, 0), (A_FORWARD, 1, 0, 1), (A_FORWARD, 1, 1, 1), (B_FORWARD, 0, 0, 1),
    (B_FORWARD, 0, 1, 1), (A_FORWARD, 2, 0, 1), (A_FORWARD, 2, 1, 1), (B_FORWARD, 1, 0, 1), (B_FORWARD, 1, 1, 1),
    (A_FORWARD, 0, 0, 2), (A_FORWARD, 0, 1, 2), (B_FORWARD, 2, 0, 1), (B_FORWARD, 2, 1, 1), (A_BEGIN, 3),
    (A_FORWARD, 1, 0, 2), (A_FORWARD, 1, 1, 2), (B_FORWARD, 0, 0, 2), (B_FORWARD, 0, 1, 2), (B_BEGIN, 3),
    (A_FORWARD, 2, 0, 2), (A_FORWARD, 2, 1, 2), (B_FORWARD, 1, 0, 2), (B_FORWARD, 1, 1, 2), (A_BEGIN, 4),
    (A_FORWARD, 0, 0, 3), (A_FORWARD, 3, 1, 0), (B_FORWARD, 2, 0, 2), (B_FORWARD, 2, 1, 2), (A_FORWARD, 1, 1, 3),
    (A_FORWARD, 3, 0, 0), (B_FORWARD, 0, 0, 3), (B_FORWARD, 3, 1, 0), (A_BEGIN, 5), (A_FORWARD, 2, 0, 3),
    (A_FORWARD, 4, 1, 0), (B_FORWARD, 1, 1, 3), (B_FORWARD, 3, 0, 0), (B_WHOLE, 0), (MULTIPLY, 0, 0),
    (A_FORWARD, 3, 1, 1), (A_FORWARD, 4, 0, 0), (B_FORWARD, 2, 0, 3), (MULTIPLY, 1, 0), (MULTIPLY, 2, 0),
    (B_FORWARD, 3, 1, 1), (B_WHOLE, 1), (MULTIPLY, 0, 1), (A_FORWARD, 3, 0, 1), (A_FORWARD, 5, 1, 0),
    (MULTIPLY, 1, 1), (MULTIPLY, 2, 1), (B_FORWARD, 3, 0, 1), (B_WHOLE, 2), (MULTIPLY, 0, 2), (A_FORWARD, 4, 1, 1),
    (A_FORWARD, 5, 0, 0), (MULTIPLY, 1, 2), (MULTIPLY, 2, 2), (A_FORWARD, 3, 1, 2), (A_FORWARD, 4, 0, 1),
    (B_FORWARD, 3, 1, 2), (B_FORWARD, 3, 0, 2), (A_FORWARD, 3, 0, 2), (A_FORWARD, 5, 1, 1), (A_FORWARD, 4, 1, 2),
    (A_FORWARD, 5, 0, 1), (B_FORWARD, 3, 1, 3), (A_FORWARD, 3, 1, 3), (A_FORWARD, 4, 0, 2), (MULTIPLY, 3, 0),
    (MULTIPLY, 3, 1), (MULTIPLY, 3, 2), (A_FORWARD, 5, 1, 2), (B_WHOLE, 3), (MULTIPLY, 0, 3), (A_FORWARD, 5, 0, 2),
    (MULTIPLY, 1, 3), (MULTIPLY, 2, 3), (MULTIPLY, 3, 3), (FINISH, 0), (A_FORWARD, 4, 0, 3), (MULTIPLY, 4, 0),
    (MULTIPLY, 4, 1), (MULTIPLY, 4, 2), (MULTIPLY, 4, 3), (A_FORWARD, 5, 1, 3), (MULTIPLY, 5, 0), (MULTIPLY, 5, 1),
    (MULTIPLY, 5, 2), (MULTIPLY, 5, 3), (FINISH, 1), (FINISH, 2), (FINISH, 3), (FINISH, 4), (FINISH, 5),
)


def hops(n, even):
    far = n // 2
    return (far, n - 1 - far) if even else (n - 1 - far, far)


def kernel(
    ny,
    nz,
    q_hbm,
    k_hbm,
    v_hbm,
    e_hbm,
    t_hbm,
    g_hbm,
    w_hbm,
    s_ref,
    o_ref,
    q_v,
    k_v,
    v_v,
    e_v,
    t_v,
    g_v,
    w_v,
    halo_out,
    halo_in,
    ext,
    taps,
    deq,
    a_buf,
    b_buf,
    c_send,
    c_recv,
    own,
    in_sem,
    halo_sem,
    a_send_sem,
    a_recv_sem,
    b_send_sem,
    b_recv_sem,
    m_send_sem,
    m_recv_sem,
    t_send_sem,
    t_recv_sem,
    c_send_sem,
    c_recv_sem,
):
    tokens, width = q_v.shape
    chunks = tokens // ROWS
    half = ROWS
    s, hid = lax.axis_index("seq"), lax.axis_index("hid")
    y, c = s // CORES, s % CORES
    z, x = hid // X, hid % X

    def at(y_, c_, z_, x_):
        return (y_ * CORES + c_, z_ * X + x_)

    z_up, z_down = at(y, c, (z + 1) % nz, x), at(y, c, (z + nz - 1) % nz, x)
    y_up, y_down = at((y + 1) % ny, c, z, x), at((y + ny - 1) % ny, c, z, x)
    sibling = at(y, 1 - c, z, x)
    seq_next = ((s + 1) % (ny * CORES), hid)

    loads = [
        pltpu.make_async_copy(src, dst, in_sem.at[n])
        for n, (src, dst) in enumerate(
            (
                (w_hbm, w_v),
                (k_hbm, k_v),
                (v_hbm, v_v),
                (t_hbm, t_v),
                (g_hbm, g_v),
                (q_hbm, q_v),
                (e_hbm, e_v),
            )
        )
    ]
    for load in loads:
        load.start()

    barrier = pltpu.get_barrier_semaphore()
    partners = [
        at(y, (c + dc) % CORES, z, (x + dx) % X)
        for dc in range(CORES)
        for dx in range(X)
        if (dc, dx) != (0, 0)
    ]
    partners += [z_up, z_down, y_up, y_down]
    partners += [at((y + ny + 2 * c - 1) % ny, 1 - c, z, x)]
    for partner in partners:
        pl.semaphore_signal(barrier, inc=1, device_id=partner, device_id_type=MESH)

    loads[1].wait()
    loads[2].wait()
    for i in range(chunks):
        rows = pl.ds(i * ROWS, ROWS)
        product = (
            k_v[rows, :].astype(jnp.float32) * v_v[rows, :].astype(jnp.float32)
        ).astype(jnp.bfloat16)
        if i == chunks - 1:
            halo_out[...] = product
        wide = product.astype(jnp.float32)
        for n in range(width // LANES):
            ext[n, pl.ds(ROWS + i * ROWS, ROWS), :] = wide[:, n * LANES : (n + 1) * LANES]

    loads[3].wait()
    loads[4].wait()
    for n in range(width // LANES):
        flat = t_v[n * LANES : (n + 1) * LANES, :].T
        taps[n] = jnp.broadcast_to(flat[:, None, :], taps.shape[1:])
        taps[n, 0] = taps[n, 0] + g_v[:, n * LANES : (n + 1) * LANES]

    loads[0].wait()
    for i in range(w_v.shape[0] // BLOCK):
        for n in range(width // BLOCK):
            rows, cols = pl.ds(i * BLOCK, BLOCK), pl.ds(n * BLOCK, BLOCK)
            deq[rows, cols] = (
                w_v[rows, cols].astype(jnp.float32) * s_ref[n, i]
            ).astype(jnp.bfloat16)

    def turn(e, core):
        here = (x == 2 * c + e) & (c == core)
        src = deq.at[pl.ds((2 * e + core) * half, half), :]
        dst = b_buf.at[x, pl.ds(pl.multiple_of((2 * y + core) * half, half), half), :]
        remote = pltpu.make_async_remote_copy(
            src_ref=src,
            dst_ref=dst,
            send_sem=t_send_sem.at[e, core],
            recv_sem=t_recv_sem.at[x],
            device_id=at(y, core, z, 2 * c + e),
            device_id_type=MESH,
        )
        local = pltpu.make_async_copy(src, dst, t_recv_sem.at[x])
        return here, remote, local

    turns = [turn(e, core) for e in range(2) for core in range(CORES)]
    halo = pltpu.make_async_remote_copy(
        src_ref=halo_out,
        dst_ref=halo_in,
        send_sem=halo_sem.at[0],
        recv_sem=halo_sem.at[1],
        device_id=seq_next,
        device_id_type=MESH,
    )
    order = [(i + 1) % chunks for i in range(chunks)]

    def preceding():
        loads[6].wait()
        halo.wait_recv()

        @pl.when(s == 0)
        def _():
            early = e_v[...].astype(jnp.float32)
            for n in range(width // LANES):
                ext[n, pl.ds(1, ROWS - 1), :] = early[:, n * LANES : (n + 1) * LANES]

        @pl.when(s != 0)
        def _():
            early = halo_in[...].astype(jnp.float32)
            for n in range(width // LANES):
                ext[n, pl.ds(0, ROWS), :] = early[:, n * LANES : (n + 1) * LANES]

    def filter_chunk(i):
        base = order[i] * ROWS
        if base == 0:
            preceding()
        tiles = ROWS // SUB
        reach = taps.shape[1] // SUB
        for n in range(width // LANES):

            def phase(b, sums):
                sums = list(sums)
                factor = [taps[n, a * SUB + b] for a in range(reach)]
                for d in range(1 - reach, tiles):
                    value = ext[n, pl.ds(ROWS + base + d * SUB - b, SUB), :]
                    for a in range(reach):
                        if 0 <= d + a < tiles:
                            sums[d + a] = sums[d + a] + factor[a] * value
                return tuple(sums)

            zero = jnp.zeros((SUB, LANES), jnp.float32)
            sums = lax.fori_loop(0, SUB, phase, (zero,) * tiles)
            filtered = jnp.concatenate(sums, axis=0)
            cols = pl.ds(n * LANES, LANES)
            a_buf[z, pl.ds(base, ROWS), cols] = (
                q_v[pl.ds(base, ROWS), cols].astype(jnp.float32) * filtered
            ).astype(jnp.bfloat16)

    loads[5].wait()
    filter_chunk(0)

    pl.semaphore_wait(barrier, len(partners))
    for here, remote, local in turns:
        pl.when(jnp.logical_not(here))(remote.start)
        pl.when(here)(local.start)
    halo.start()

    def a_copy(i, way, hop):
        step = 1 if way == 0 else -1
        block = a_buf.at[(z + nz - step * hop) % nz, pl.ds(order[i] * ROWS, ROWS), :]
        return pltpu.make_async_remote_copy(
            src_ref=block,
            dst_ref=block,
            send_sem=a_send_sem,
            recv_sem=a_recv_sem.at[i, way, hop],
            device_id=z_up if way == 0 else z_down,
            device_id_type=MESH,
        )

    def a_arrived(i, way, hop):
        step = 1 if way == 0 else -1
        block = a_buf.at[
            (z + nz - step * (hop + 1)) % nz, pl.ds(order[i] * ROWS, ROWS), :
        ]
        pltpu.make_async_copy(block, block, a_recv_sem.at[i, way, hop]).wait()

    def a_forward(i, way, hop):
        a_arrived(i, way, hop)
        if hop + 1 < hops(nz, i % 2 == 0)[way]:
            a_copy(i, way, hop + 1).start()

    def piece_column(p):
        return (x + (2, 1, 3, 0)[p]) % X

    def b_block(p, owner, core):
        rows = pl.ds(pl.multiple_of((2 * owner + core) * half, half), half)
        return b_buf.at[piece_column(p), rows, :]

    def b_copy(p, way, hop):
        step = 1 if way == 0 else -1
        block = b_block(p, (y + ny - step * hop) % ny, c)
        return pltpu.make_async_remote_copy(
            src_ref=block,
            dst_ref=block,
            send_sem=b_send_sem,
            recv_sem=b_recv_sem.at[p, way, hop],
            device_id=y_up if way == 0 else y_down,
            device_id_type=MESH,
        )

    def to_sibling(p, owner):
        block = b_block(p, owner, c)
        pltpu.make_async_remote_copy(
            src_ref=block,
            dst_ref=block,
            send_sem=m_send_sem,
            recv_sem=m_recv_sem.at[p, owner],
            device_id=sibling,
            device_id_type=MESH,
        ).start()

    def b_start(p):
        column = piece_column(p)
        block = b_block(p, y, c)
        pltpu.make_async_copy(block, block, t_recv_sem.at[column]).wait()
        for way in range(2):
            if hops(ny, p % 2 == 0)[way]:
                b_copy(p, way, 0).start()
        to_sibling(p, y)

    def b_forward(p, way, hop):
        step = 1 if way == 0 else -1
        owner = (y + ny - step * (hop + 1)) % ny
        block = b_block(p, owner, c)
        pltpu.make_async_copy(block, block, b_recv_sem.at[p, way, hop]).wait()
        if hop + 1 < hops(ny, p % 2 == 0)[way]:
            b_copy(p, way, hop + 1).start()
        to_sibling(p, owner)

    def b_whole(p):
        for owner in range(ny):
            block = b_block(p, owner, 1 - c)
            pltpu.make_async_copy(block, block, m_recv_sem.at[p, owner]).wait()

    def multiply(i, p):
        rows = pl.ds(order[i] * ROWS, ROWS)
        left = jnp.concatenate([a_buf[k, rows, :] for k in range(nz)], axis=1)
        total = jnp.dot(
            left, b_buf[piece_column(p)], preferred_element_type=jnp.float32
        )
        if p == X - 1:
            own[rows, :] = total
            return
        c_send[p, rows, :] = total.astype(jnp.bfloat16)
        pltpu.make_async_remote_copy(
            src_ref=c_send.at[p, rows, :],
            dst_ref=c_recv.at[p, rows, :],
            send_sem=c_send_sem,
            recv_sem=c_recv_sem.at[i, p],
            device_id=at(y, c, z, piece_column(p)),
            device_id_type=MESH,
        ).start()

    def finish(i):
        rows = pl.ds(order[i] * ROWS, ROWS)
        total = own[rows, :]
        for p in range(X - 1):
            block = c_recv.at[p, rows, :]
            pltpu.make_async_copy(block, block, c_recv_sem.at[i, p]).wait()
            total = total + c_recv[p, rows, :].astype(jnp.float32)
        o_ref[rows, :] = total.astype(jnp.bfloat16)

    def a_begin(i):
        for way in range(2):
            if hops(nz, i % 2 == 0)[way]:
                a_copy(i, way, 0).start()

    work = {
        FILTER: filter_chunk,
        A_BEGIN: a_begin,
        A_FORWARD: a_forward,
        B_BEGIN: b_start,
        B_FORWARD: b_forward,
        B_WHOLE: b_whole,
        MULTIPLY: multiply,
        FINISH: finish,
    }
    for name, *where in PLAN:
        work[name](*where)

    for here, remote, local in turns:
        pl.when(jnp.logical_not(here))(remote.wait_send)
    halo.wait_send()
    sent = a_buf.at[pl.ds(0, nz - 1)]
    pltpu.make_async_copy(sent, sent, a_send_sem).wait()
    sent = b_buf.at[:, pl.ds(0, (ny - 1) * half), :]
    pltpu.make_async_copy(sent, sent, b_send_sem).wait()
    sent = b_buf.at[:, pl.ds(0, ny * half), :]
    pltpu.make_async_copy(sent, sent, m_send_sem).wait()
    pltpu.make_async_copy(c_send, c_send, c_send_sem).wait()


def on_device(ny, nz, q, k, v, earlier, taps, gain, weight, scales):
    tokens, width = q.shape
    depth = weight.shape[0]
    reach = taps.shape[1]
    chunks = tokens // ROWS
    vmem, dma = pltpu.VMEM, pltpu.SemaphoreType.DMA
    bf16, f32 = jnp.bfloat16, jnp.float32
    anywhere = pl.BlockSpec(memory_space=pltpu.HBM)
    gain = gain.reshape(1, width)
    return pl.pallas_call(
        functools.partial(kernel, ny, nz),
        out_shape=jax.ShapeDtypeStruct((tokens, width), bf16),
        in_specs=[anywhere] * 7 + [pl.BlockSpec(memory_space=pltpu.SMEM)],
        out_specs=pl.BlockSpec(memory_space=pltpu.VMEM),
        scratch_shapes=[
            vmem(q.shape, bf16),
            vmem(k.shape, bf16),
            vmem(v.shape, bf16),
            vmem(earlier.shape, bf16),
            vmem(taps.shape, f32),
            vmem(gain.shape, f32),
            vmem(weight.shape, bf16),
            vmem((ROWS, width), bf16),
            vmem((ROWS, width), bf16),
            vmem((width // LANES, ROWS + tokens, LANES), f32),
            vmem((width // LANES, reach, SUB, LANES), f32),
            vmem((depth, width), bf16),
            vmem((nz, tokens, width), bf16),
            vmem((X, nz * width, width), bf16),
            vmem((X - 1, tokens, width), bf16),
            vmem((X - 1, tokens, width), bf16),
            vmem((tokens, width), f32),
            dma((7,)),
            dma((2,)),
            dma,
            dma((chunks, 2, nz // 2)),
            dma,
            dma((X, 2, ny // 2)),
            dma,
            dma((X, ny)),
            dma((2, CORES)),
            dma((X,)),
            dma,
            dma((chunks, X - 1)),
        ],
        compiler_params=pltpu.CompilerParams(
            collective_id=0, has_side_effects=True, vmem_limit_bytes=63 * 1024 * 1024
        ),
        cost_estimate=pl.CostEstimate(
            flops=2 * tokens * nz * width * X * width,
            bytes_accessed=4 * tokens * width * 2,
            transcendentals=0,
        ),
    )(q, k, v, earlier, taps, gain, weight, scales.T)


def solution(mesh):
    ny = mesh.shape["seq"] // CORES
    nz = mesh.shape["hid"] // X
    return jax.shard_map(
        functools.partial(on_device, ny, nz),
        mesh=mesh,
        in_specs=(
            P("seq", "hid"),
            P("seq", "hid"),
            P("seq", "hid"),
            P(None, "hid"),
            P("hid", None),
            P("hid"),
            P("seq", "hid"),
            P("seq", "hid"),
        ),
        out_specs=P("seq", "hid"),
        check_vma=False,
    )
```

```python
import functools

import jax
import jax.numpy as jnp
from jax import lax
from jax.experimental import pallas as pl
from jax.experimental.pallas import tpu as pltpu
from jax.sharding import PartitionSpec as P

MESH = pl.DeviceIdType.MESH
X = 4
CORES = 2
BLOCK = 128
LANES = 128
SUB = 8
ROWS = 128
FILTER, A_BEGIN, A_FORWARD, B_BEGIN, B_FORWARD, B_WHOLE, MULTIPLY, FINISH = range(8)
PLAN = (
    (A_BEGIN, 0), (FILTER, 1), (B_BEGIN, 0), (A_BEGIN, 1), (FILTER, 2), (B_BEGIN, 1), (A_BEGIN, 2), (FILTER, 3),
    (A_FORWARD, 0, 0, 0), (A_FORWARD, 0, 1, 0), (B_BEGIN, 2), (B_FORWARD, 0, 0, 0), (A_FORWARD, 1, 0, 0),
    (A_FORWARD, 1, 1, 0), (B_FORWARD, 0, 1, 0), (FILTER, 4), (B_FORWARD, 1, 0, 0), (A_FORWARD, 2, 0, 0),
    (A_FORWARD, 2, 1, 0), (B_FORWARD, 1, 1, 0), (FILTER, 5), (A_FORWARD, 0, 0, 1), (A_FORWARD, 0, 1, 1),
    (B_FORWARD, 2, 0, 0), (B_FORWARD, 2, 1, 0), (A_FORWARD, 1, 0, 1), (A_FORWARD, 1, 1, 1), (B_FORWARD, 0, 0, 1),
    (B_FORWARD, 0, 1, 1), (A_FORWARD, 2, 0, 1), (A_FORWARD, 2, 1, 1), (B_FORWARD, 1, 0, 1), (B_FORWARD, 1, 1, 1),
    (A_FORWARD, 0, 0, 2), (A_FORWARD, 0, 1, 2), (B_FORWARD, 2, 0, 1), (B_FORWARD, 2, 1, 1), (A_BEGIN, 3),
    (A_FORWARD, 1, 0, 2), (A_FORWARD, 1, 1, 2), (B_FORWARD, 0, 0, 2), (B_FORWARD, 0, 1, 2), (B_BEGIN, 3),
    (A_FORWARD, 2, 0, 2), (A_FORWARD, 2, 1, 2), (B_FORWARD, 1, 0, 2), (B_FORWARD, 1, 1, 2), (A_BEGIN, 4),
    (A_FORWARD, 0, 0, 3), (A_FORWARD, 3, 1, 0), (B_FORWARD, 2, 0, 2), (B_FORWARD, 2, 1, 2), (A_FORWARD, 1, 1, 3),
    (A_FORWARD, 3, 0, 0), (B_FORWARD, 0, 0, 3), (B_FORWARD, 3, 1, 0), (A_BEGIN, 5), (A_FORWARD, 2, 0, 3),
    (A_FORWARD, 4, 1, 0), (B_FORWARD, 1, 1, 3), (B_FORWARD, 3, 0, 0), (B_WHOLE, 0), (MULTIPLY, 0, 0),
    (A_FORWARD, 3, 1, 1), (A_FORWARD, 4, 0, 0), (B_FORWARD, 2, 0, 3), (MULTIPLY, 1, 0), (MULTIPLY, 2, 0),
    (B_FORWARD, 3, 1, 1), (B_WHOLE, 1), (MULTIPLY, 0, 1), (A_FORWARD, 3, 0, 1), (A_FORWARD, 5, 1, 0),
    (MULTIPLY, 1, 1), (MULTIPLY, 2, 1), (B_FORWARD, 3, 0, 1), (B_WHOLE, 2), (MULTIPLY, 0, 2), (A_FORWARD, 4, 1, 1),
    (A_FORWARD, 5, 0, 0), (MULTIPLY, 1, 2), (MULTIPLY, 2, 2), (A_FORWARD, 3, 1, 2), (A_FORWARD, 4, 0, 1),
    (B_FORWARD, 3, 1, 2), (B_FORWARD, 3, 0, 2), (A_FORWARD, 3, 0, 2), (A_FORWARD, 5, 1, 1), (A_FORWARD, 4, 1, 2),
    (A_FORWARD, 5, 0, 1), (B_FORWARD, 3, 1, 3), (A_FORWARD, 3, 1, 3), (A_FORWARD, 4, 0, 2), (MULTIPLY, 3, 0),
    (MULTIPLY, 3, 1), (MULTIPLY, 3, 2), (A_FORWARD, 5, 1, 2), (B_WHOLE, 3), (MULTIPLY, 0, 3), (A_FORWARD, 5, 0, 2),
    (MULTIPLY, 1, 3), (MULTIPLY, 2, 3), (MULTIPLY, 3, 3), (FINISH, 0), (A_FORWARD, 4, 0, 3), (MULTIPLY, 4, 0),
    (MULTIPLY, 4, 1), (MULTIPLY, 4, 2), (MULTIPLY, 4, 3), (A_FORWARD, 5, 1, 3), (MULTIPLY, 5, 0), (MULTIPLY, 5, 1),
    (MULTIPLY, 5, 2), (MULTIPLY, 5, 3), (FINISH, 1), (FINISH, 2), (FINISH, 3), (FINISH, 4), (FINISH, 5),
)


def hops(n, even):
    far = n // 2
    return (far, n - 1 - far) if even else (n - 1 - far, far)


def kernel(
    ny,
    nz,
    q_hbm,
    k_hbm,
    v_hbm,
    e_hbm,
    t_hbm,
    g_hbm,
    w_hbm,
    s_ref,
    o_ref,
    q_v,
    k_v,
    v_v,
    e_v,
    t_v,
    g_v,
    w_v,
    halo_out,
    halo_in,
    ext,
    taps,
    deq,
    a_buf,
    b_buf,
    c_send,
    c_recv,
    own,
    in_sem,
    halo_sem,
    a_send_sem,
    a_recv_sem,
    b_send_sem,
    b_recv_sem,
    m_send_sem,
    m_recv_sem,
    t_send_sem,
    t_recv_sem,
    c_send_sem,
    c_recv_sem,
):
    tokens, width = q_v.shape
    chunks = tokens // ROWS
    half = ROWS
    s, hid = lax.axis_index("seq"), lax.axis_index("hid")
    y, c = s // CORES, s % CORES
    z, x = hid // X, hid % X

    def at(y_, c_, z_, x_):
        return (y_ * CORES + c_, z_ * X + x_)

    z_up, z_down = at(y, c, (z + 1) % nz, x), at(y, c, (z + nz - 1) % nz, x)
    y_up, y_down = at((y + 1) % ny, c, z, x), at((y + ny - 1) % ny, c, z, x)
    sibling = at(y, 1 - c, z, x)
    seq_next = ((s + 1) % (ny * CORES), hid)

    barrier = pltpu.get_barrier_semaphore()
    partners = [z_up, z_down, y_up, y_down]
    partners += [
        at(y, (c + dc) % CORES, z, (x + dx) % X)
        for dc in range(CORES)
        for dx in range(X)
        if (dc, dx) != (0, 0)
    ]
    partners += [at((y + ny + 2 * c - 1) % ny, 1 - c, z, x)]
    for partner in partners:
        pl.semaphore_signal(barrier, inc=1, device_id=partner, device_id_type=MESH)

    loads = [
        pltpu.make_async_copy(src, dst, in_sem.at[n])
        for n, (src, dst) in enumerate(
            (
                (w_hbm, w_v),
                (k_hbm, k_v),
                (v_hbm, v_v),
                (t_hbm, t_v),
                (g_hbm, g_v),
                (q_hbm, q_v),
                (e_hbm, e_v),
            )
        )
    ]
    for load in loads:
        load.start()

    loads[0].wait()
    for i in range(w_v.shape[0] // BLOCK):
        for n in range(width // BLOCK):
            rows, cols = pl.ds(i * BLOCK, BLOCK), pl.ds(n * BLOCK, BLOCK)
            deq[rows, cols] = (
                w_v[rows, cols].astype(jnp.float32) * s_ref[n, i]
            ).astype(jnp.bfloat16)

    def turn(e, core):
        here = (x == 2 * c + e) & (c == core)
        src = deq.at[pl.ds((2 * e + core) * half, half), :]
        dst = b_buf.at[x, pl.ds(pl.multiple_of((2 * y + core) * half, half), half), :]
        remote = pltpu.make_async_remote_copy(
            src_ref=src,
            dst_ref=dst,
            send_sem=t_send_sem.at[e, core],
            recv_sem=t_recv_sem.at[x],
            device_id=at(y, core, z, 2 * c + e),
            device_id_type=MESH,
        )
        local = pltpu.make_async_copy(src, dst, t_recv_sem.at[x])
        return here, remote, local

    turns = [turn(e, core) for e in range(2) for core in range(CORES)]
    pl.semaphore_wait(barrier, len(partners))
    for here, remote, local in turns:
        pl.when(jnp.logical_not(here))(remote.start)
        pl.when(here)(local.start)

    loads[1].wait()
    loads[2].wait()
    for i in range(chunks):
        rows = pl.ds(i * ROWS, ROWS)
        product = (
            k_v[rows, :].astype(jnp.float32) * v_v[rows, :].astype(jnp.float32)
        ).astype(jnp.bfloat16)
        if i == chunks - 1:
            halo_out[...] = product
        wide = product.astype(jnp.float32)
        for n in range(width // LANES):
            ext[n, pl.ds(ROWS + i * ROWS, ROWS), :] = wide[:, n * LANES : (n + 1) * LANES]

    halo = pltpu.make_async_remote_copy(
        src_ref=halo_out,
        dst_ref=halo_in,
        send_sem=halo_sem.at[0],
        recv_sem=halo_sem.at[1],
        device_id=seq_next,
        device_id_type=MESH,
    )
    halo.start()

    order = [(i + 1) % chunks for i in range(chunks)]

    def preceding():
        loads[6].wait()
        halo.wait_recv()

        @pl.when(s == 0)
        def _():
            early = e_v[...].astype(jnp.float32)
            for n in range(width // LANES):
                ext[n, pl.ds(1, ROWS - 1), :] = early[:, n * LANES : (n + 1) * LANES]

        @pl.when(s != 0)
        def _():
            early = halo_in[...].astype(jnp.float32)
            for n in range(width // LANES):
                ext[n, pl.ds(0, ROWS), :] = early[:, n * LANES : (n + 1) * LANES]

    def filter_chunk(i):
        base = order[i] * ROWS
        if base == 0:
            preceding()
        tiles = ROWS // SUB
        reach = taps.shape[1] // SUB
        for n in range(width // LANES):

            def phase(b, sums):
                sums = list(sums)
                factor = [taps[n, a * SUB + b] for a in range(reach)]
                for d in range(1 - reach, tiles):
                    value = ext[n, pl.ds(ROWS + base + d * SUB - b, SUB), :]
                    for a in range(reach):
                        if 0 <= d + a < tiles:
                            sums[d + a] = sums[d + a] + factor[a] * value
                return tuple(sums)

            zero = jnp.zeros((SUB, LANES), jnp.float32)
            sums = lax.fori_loop(0, SUB, phase, (zero,) * tiles)
            filtered = jnp.concatenate(sums, axis=0)
            cols = pl.ds(n * LANES, LANES)
            a_buf[z, pl.ds(base, ROWS), cols] = (
                q_v[pl.ds(base, ROWS), cols].astype(jnp.float32) * filtered
            ).astype(jnp.bfloat16)

    loads[3].wait()
    loads[4].wait()
    for n in range(width // LANES):
        flat = t_v[n * LANES : (n + 1) * LANES, :].T
        taps[n] = jnp.broadcast_to(flat[:, None, :], taps.shape[1:])
        taps[n, 0] = taps[n, 0] + g_v[:, n * LANES : (n + 1) * LANES]

    loads[5].wait()
    filter_chunk(0)

    def a_copy(i, way, hop):
        step = 1 if way == 0 else -1
        block = a_buf.at[(z + nz - step * hop) % nz, pl.ds(order[i] * ROWS, ROWS), :]
        return pltpu.make_async_remote_copy(
            src_ref=block,
            dst_ref=block,
            send_sem=a_send_sem,
            recv_sem=a_recv_sem.at[i, way, hop],
            device_id=z_up if way == 0 else z_down,
            device_id_type=MESH,
        )

    def a_arrived(i, way, hop):
        step = 1 if way == 0 else -1
        block = a_buf.at[
            (z + nz - step * (hop + 1)) % nz, pl.ds(order[i] * ROWS, ROWS), :
        ]
        pltpu.make_async_copy(block, block, a_recv_sem.at[i, way, hop]).wait()

    def a_forward(i, way, hop):
        a_arrived(i, way, hop)
        if hop + 1 < hops(nz, i % 2 == 0)[way]:
            a_copy(i, way, hop + 1).start()

    def piece_column(p):
        return (x + (2, 1, 3, 0)[p]) % X

    def b_block(p, owner, core):
        rows = pl.ds(pl.multiple_of((2 * owner + core) * half, half), half)
        return b_buf.at[piece_column(p), rows, :]

    def b_copy(p, way, hop):
        step = 1 if way == 0 else -1
        block = b_block(p, (y + ny - step * hop) % ny, c)
        return pltpu.make_async_remote_copy(
            src_ref=block,
            dst_ref=block,
            send_sem=b_send_sem,
            recv_sem=b_recv_sem.at[p, way, hop],
            device_id=y_up if way == 0 else y_down,
            device_id_type=MESH,
        )

    def to_sibling(p, owner):
        block = b_block(p, owner, c)
        pltpu.make_async_remote_copy(
            src_ref=block,
            dst_ref=block,
            send_sem=m_send_sem,
            recv_sem=m_recv_sem.at[p, owner],
            device_id=sibling,
            device_id_type=MESH,
        ).start()

    def b_start(p):
        column = piece_column(p)
        block = b_block(p, y, c)
        pltpu.make_async_copy(block, block, t_recv_sem.at[column]).wait()
        for way in range(2):
            if hops(ny, p % 2 == 0)[way]:
                b_copy(p, way, 0).start()
        to_sibling(p, y)

    def b_forward(p, way, hop):
        step = 1 if way == 0 else -1
        owner = (y + ny - step * (hop + 1)) % ny
        block = b_block(p, owner, c)
        pltpu.make_async_copy(block, block, b_recv_sem.at[p, way, hop]).wait()
        if hop + 1 < hops(ny, p % 2 == 0)[way]:
            b_copy(p, way, hop + 1).start()
        to_sibling(p, owner)

    def b_whole(p):
        for owner in range(ny):
            block = b_block(p, owner, 1 - c)
            pltpu.make_async_copy(block, block, m_recv_sem.at[p, owner]).wait()

    def multiply(i, p):
        rows = pl.ds(order[i] * ROWS, ROWS)
        left = jnp.concatenate([a_buf[k, rows, :] for k in range(nz)], axis=1)
        total = jnp.dot(
            left, b_buf[piece_column(p)], preferred_element_type=jnp.float32
        )
        if p == X - 1:
            own[rows, :] = total
            return
        c_send[p, rows, :] = total.astype(jnp.bfloat16)
        pltpu.make_async_remote_copy(
            src_ref=c_send.at[p, rows, :],
            dst_ref=c_recv.at[p, rows, :],
            send_sem=c_send_sem,
            recv_sem=c_recv_sem.at[i, p],
            device_id=at(y, c, z, piece_column(p)),
            device_id_type=MESH,
        ).start()

    def finish(i):
        rows = pl.ds(order[i] * ROWS, ROWS)
        total = own[rows, :]
        for p in range(X - 1):
            block = c_recv.at[p, rows, :]
            pltpu.make_async_copy(block, block, c_recv_sem.at[i, p]).wait()
            total = total + c_recv[p, rows, :].astype(jnp.float32)
        o_ref[rows, :] = total.astype(jnp.bfloat16)

    def a_begin(i):
        for way in range(2):
            if hops(nz, i % 2 == 0)[way]:
                a_copy(i, way, 0).start()

    work = {
        FILTER: filter_chunk,
        A_BEGIN: a_begin,
        A_FORWARD: a_forward,
        B_BEGIN: b_start,
        B_FORWARD: b_forward,
        B_WHOLE: b_whole,
        MULTIPLY: multiply,
        FINISH: finish,
    }
    for name, *where in PLAN:
        work[name](*where)

    for here, remote, local in turns:
        pl.when(jnp.logical_not(here))(remote.wait_send)
    halo.wait_send()
    sent = a_buf.at[pl.ds(0, nz - 1)]
    pltpu.make_async_copy(sent, sent, a_send_sem).wait()
    sent = b_buf.at[:, pl.ds(0, (ny - 1) * half), :]
    pltpu.make_async_copy(sent, sent, b_send_sem).wait()
    sent = b_buf.at[:, pl.ds(0, ny * half), :]
    pltpu.make_async_copy(sent, sent, m_send_sem).wait()
    pltpu.make_async_copy(c_send, c_send, c_send_sem).wait()


def on_device(ny, nz, q, k, v, earlier, taps, gain, weight, scales):
    tokens, width = q.shape
    depth = weight.shape[0]
    reach = taps.shape[1]
    chunks = tokens // ROWS
    vmem, dma = pltpu.VMEM, pltpu.SemaphoreType.DMA
    bf16, f32 = jnp.bfloat16, jnp.float32
    anywhere = pl.BlockSpec(memory_space=pltpu.HBM)
    gain = gain.reshape(1, width)
    return pl.pallas_call(
        functools.partial(kernel, ny, nz),
        out_shape=pltpu.VMEM((tokens, width), bf16),
        in_specs=[anywhere] * 7 + [pl.BlockSpec(memory_space=pltpu.SMEM)],
        out_specs=pl.BlockSpec(memory_space=pltpu.VMEM),
        scratch_shapes=[
            vmem(q.shape, bf16),
            vmem(k.shape, bf16),
            vmem(v.shape, bf16),
            vmem(earlier.shape, bf16),
            vmem(taps.shape, f32),
            vmem(gain.shape, f32),
            vmem(weight.shape, bf16),
            vmem((ROWS, width), bf16),
            vmem((ROWS, width), bf16),
            vmem((width // LANES, ROWS + tokens, LANES), f32),
            vmem((width // LANES, reach, SUB, LANES), f32),
            vmem((depth, width), bf16),
            vmem((nz, tokens, width), bf16),
            vmem((X, nz * width, width), bf16),
            vmem((X - 1, tokens, width), bf16),
            vmem((X - 1, tokens, width), bf16),
            vmem((tokens, width), f32),
            dma((7,)),
            dma((2,)),
            dma,
            dma((chunks, 2, nz // 2)),
            dma,
            dma((X, 2, ny // 2)),
            dma,
            dma((X, ny)),
            dma((2, CORES)),
            dma((X,)),
            dma,
            dma((chunks, X - 1)),
        ],
        compiler_params=pltpu.CompilerParams(
            collective_id=0, has_side_effects=True, vmem_limit_bytes=63 * 1024 * 1024
        ),
        cost_estimate=pl.CostEstimate(
            flops=2 * tokens * nz * width * X * width,
            bytes_accessed=4 * tokens * width * 2,
            transcendentals=0,
        ),
    )(q, k, v, earlier, taps, gain, weight, scales.T)


def solution(mesh):
    ny = mesh.shape["seq"] // CORES
    nz = mesh.shape["hid"] // X
    return jax.shard_map(
        functools.partial(on_device, ny, nz),
        mesh=mesh,
        in_specs=(
            P("seq", "hid"),
            P("seq", "hid"),
            P("seq", "hid"),
            P(None, "hid"),
            P("hid", None),
            P("hid"),
            P("seq", "hid"),
            P("seq", "hid"),
        ),
        out_specs=P("seq", "hid"),
        check_vma=False,
    )
```

```python
import functools

import jax
import jax.numpy as jnp
from jax import lax
from jax.experimental import pallas as pl
from jax.experimental.pallas import tpu as pltpu
from jax.sharding import PartitionSpec as P

MESH = pl.DeviceIdType.MESH
X = 4
CORES = 2
BLOCK = 128
LANES = 128
SUB = 8
ROWS = 128
FILTER, A_BEGIN, A_FORWARD, B_BEGIN, B_FORWARD, B_WHOLE, MULTIPLY, FINISH = range(8)
PLAN = (
    (A_BEGIN, 0), (FILTER, 1), (B_BEGIN, 0), (A_BEGIN, 1), (FILTER, 2), (B_BEGIN, 1), (A_BEGIN, 2), (FILTER, 3),
    (A_FORWARD, 0, 0, 0), (A_FORWARD, 0, 1, 0), (B_BEGIN, 2), (B_FORWARD, 0, 0, 0), (A_FORWARD, 1, 0, 0),
    (A_FORWARD, 1, 1, 0), (B_FORWARD, 0, 1, 0), (FILTER, 4), (B_FORWARD, 1, 0, 0), (A_FORWARD, 2, 0, 0),
    (A_FORWARD, 2, 1, 0), (B_FORWARD, 1, 1, 0), (FILTER, 5), (A_FORWARD, 0, 0, 1), (A_FORWARD, 0, 1, 1),
    (B_FORWARD, 2, 0, 0), (B_FORWARD, 2, 1, 0), (A_FORWARD, 1, 0, 1), (A_FORWARD, 1, 1, 1), (B_FORWARD, 0, 0, 1),
    (B_FORWARD, 0, 1, 1), (A_FORWARD, 2, 0, 1), (A_FORWARD, 2, 1, 1), (B_FORWARD, 1, 0, 1), (B_FORWARD, 1, 1, 1),
    (A_FORWARD, 0, 0, 2), (A_FORWARD, 0, 1, 2), (B_FORWARD, 2, 0, 1), (B_FORWARD, 2, 1, 1), (A_BEGIN, 3),
    (A_FORWARD, 1, 0, 2), (A_FORWARD, 1, 1, 2), (B_FORWARD, 0, 0, 2), (B_FORWARD, 0, 1, 2), (B_BEGIN, 3),
    (B_FORWARD, 1, 0, 2), (A_FORWARD, 2, 0, 2), (B_FORWARD, 1, 1, 2), (A_FORWARD, 2, 1, 2), (A_BEGIN, 4),
    (A_FORWARD, 0, 0, 3), (A_FORWARD, 3, 1, 0), (B_FORWARD, 2, 0, 2), (B_FORWARD, 2, 1, 2), (A_FORWARD, 1, 1, 3),
    (A_FORWARD, 3, 0, 0), (B_FORWARD, 0, 0, 3), (B_FORWARD, 3, 1, 0), (A_BEGIN, 5), (A_FORWARD, 2, 0, 3),
    (A_FORWARD, 4, 1, 0), (B_FORWARD, 1, 1, 3), (B_FORWARD, 2, 0, 3), (B_FORWARD, 3, 0, 0), (B_WHOLE, 0),
    (MULTIPLY, 0, 0), (A_FORWARD, 3, 1, 1), (A_FORWARD, 4, 0, 0), (MULTIPLY, 1, 0), (MULTIPLY, 2, 0),
    (B_FORWARD, 3, 1, 1), (B_WHOLE, 1), (MULTIPLY, 0, 1), (A_FORWARD, 3, 0, 1), (A_FORWARD, 5, 1, 0),
    (MULTIPLY, 1, 1), (MULTIPLY, 2, 1), (B_FORWARD, 3, 0, 1), (B_WHOLE, 2), (MULTIPLY, 0, 2), (A_FORWARD, 4, 1, 1),
    (A_FORWARD, 5, 0, 0), (MULTIPLY, 1, 2), (MULTIPLY, 2, 2), (A_FORWARD, 3, 1, 2), (A_FORWARD, 4, 0, 1),
    (B_FORWARD, 3, 1, 2), (B_FORWARD, 3, 0, 2), (A_FORWARD, 3, 0, 2), (A_FORWARD, 5, 1, 1), (A_FORWARD, 4, 1, 2),
    (A_FORWARD, 5, 0, 1), (B_FORWARD, 3, 1, 3), (A_FORWARD, 3, 1, 3), (A_FORWARD, 4, 0, 2), (MULTIPLY, 3, 0),
    (MULTIPLY, 3, 1), (MULTIPLY, 3, 2), (A_FORWARD, 5, 1, 2), (B_WHOLE, 3), (MULTIPLY, 0, 3), (A_FORWARD, 5, 0, 2),
    (MULTIPLY, 1, 3), (MULTIPLY, 2, 3), (MULTIPLY, 3, 3), (A_FORWARD, 5, 1, 3), (FINISH, 0), (A_FORWARD, 4, 0, 3),
    (MULTIPLY, 4, 0), (MULTIPLY, 4, 1), (MULTIPLY, 4, 2), (MULTIPLY, 4, 3), (MULTIPLY, 5, 0), (MULTIPLY, 5, 1),
    (MULTIPLY, 5, 2), (MULTIPLY, 5, 3), (FINISH, 1), (FINISH, 2), (FINISH, 3), (FINISH, 4), (FINISH, 5),
)


def hops(n, even):
    far = n // 2
    return (far, n - 1 - far) if even else (n - 1 - far, far)


def kernel(
    ny,
    nz,
    q_hbm,
    k_hbm,
    v_hbm,
    e_hbm,
    t_hbm,
    g_hbm,
    w_hbm,
    s_ref,
    o_ref,
    q_v,
    k_v,
    v_v,
    e_v,
    t_v,
    g_v,
    w_v,
    halo_out,
    halo_in,
    ext,
    taps,
    deq,
    a_buf,
    b_buf,
    c_send,
    c_recv,
    own,
    in_sem,
    halo_sem,
    a_send_sem,
    a_recv_sem,
    b_send_sem,
    b_recv_sem,
    m_send_sem,
    m_recv_sem,
    t_send_sem,
    t_recv_sem,
    c_send_sem,
    c_recv_sem,
):
    tokens, width = q_v.shape
    chunks = tokens // ROWS
    half = ROWS
    s, hid = lax.axis_index("seq"), lax.axis_index("hid")
    y, c = s // CORES, s % CORES
    z, x = hid // X, hid % X

    def at(y_, c_, z_, x_):
        return (y_ * CORES + c_, z_ * X + x_)

    z_up, z_down = at(y, c, (z + 1) % nz, x), at(y, c, (z + nz - 1) % nz, x)
    y_up, y_down = at((y + 1) % ny, c, z, x), at((y + ny - 1) % ny, c, z, x)
    sibling = at(y, 1 - c, z, x)
    seq_next = ((s + 1) % (ny * CORES), hid)

    barrier = pltpu.get_barrier_semaphore()
    partners = [z_up, z_down, y_up, y_down]
    partners += [
        at(y, (c + dc) % CORES, z, (x + dx) % X)
        for dc in range(CORES)
        for dx in range(X)
        if (dc, dx) != (0, 0)
    ]
    partners += [at((y + ny + 2 * c - 1) % ny, 1 - c, z, x)]
    for partner in partners:
        pl.semaphore_signal(barrier, inc=1, device_id=partner, device_id_type=MESH)

    loads = [
        pltpu.make_async_copy(src, dst, in_sem.at[n])
        for n, (src, dst) in enumerate(
            (
                (w_hbm, w_v),
                (k_hbm, k_v),
                (v_hbm, v_v),
                (t_hbm, t_v),
                (g_hbm, g_v),
                (q_hbm, q_v),
                (e_hbm, e_v),
            )
        )
    ]
    for load in loads:
        load.start()

    loads[0].wait()
    for i in range(w_v.shape[0] // BLOCK):
        for n in range(width // BLOCK):
            rows, cols = pl.ds(i * BLOCK, BLOCK), pl.ds(n * BLOCK, BLOCK)
            deq[rows, cols] = (
                w_v[rows, cols].astype(jnp.float32) * s_ref[n, i]
            ).astype(jnp.bfloat16)

    def turn(e, core):
        here = (x == 2 * c + e) & (c == core)
        src = deq.at[pl.ds((2 * e + core) * half, half), :]
        dst = b_buf.at[x, pl.ds(pl.multiple_of((2 * y + core) * half, half), half), :]
        remote = pltpu.make_async_remote_copy(
            src_ref=src,
            dst_ref=dst,
            send_sem=t_send_sem.at[e, core],
            recv_sem=t_recv_sem.at[x],
            device_id=at(y, core, z, 2 * c + e),
            device_id_type=MESH,
        )
        local = pltpu.make_async_copy(src, dst, t_recv_sem.at[x])
        return here, remote, local

    turns = [turn(e, core) for e in range(2) for core in range(CORES)]
    pl.semaphore_wait(barrier, len(partners))
    for here, remote, local in turns:
        pl.when(jnp.logical_not(here))(remote.start)
        pl.when(here)(local.start)

    loads[1].wait()
    loads[2].wait()
    for i in range(chunks):
        rows = pl.ds(i * ROWS, ROWS)
        product = (
            k_v[rows, :].astype(jnp.float32) * v_v[rows, :].astype(jnp.float32)
        ).astype(jnp.bfloat16)
        if i == chunks - 1:
            halo_out[...] = product
        wide = product.astype(jnp.float32)
        for n in range(width // LANES):
            ext[n, pl.ds(ROWS + i * ROWS, ROWS), :] = wide[:, n * LANES : (n + 1) * LANES]

    halo = pltpu.make_async_remote_copy(
        src_ref=halo_out,
        dst_ref=halo_in,
        send_sem=halo_sem.at[0],
        recv_sem=halo_sem.at[1],
        device_id=seq_next,
        device_id_type=MESH,
    )
    halo.start()

    order = [(i + 1) % chunks for i in range(chunks)]

    def preceding():
        loads[6].wait()
        halo.wait_recv()

        @pl.when(s == 0)
        def _():
            early = e_v[...].astype(jnp.float32)
            for n in range(width // LANES):
                ext[n, pl.ds(1, ROWS - 1), :] = early[:, n * LANES : (n + 1) * LANES]

        @pl.when(s != 0)
        def _():
            early = halo_in[...].astype(jnp.float32)
            for n in range(width // LANES):
                ext[n, pl.ds(0, ROWS), :] = early[:, n * LANES : (n + 1) * LANES]

    def filter_chunk(i):
        base = order[i] * ROWS
        if base == 0:
            preceding()
        tiles = ROWS // SUB
        reach = taps.shape[1] // SUB
        for n in range(width // LANES):

            def phase(b, sums):
                sums = list(sums)
                factor = [taps[n, a * SUB + b] for a in range(reach)]
                for d in range(1 - reach, tiles):
                    value = ext[n, pl.ds(ROWS + base + d * SUB - b, SUB), :]
                    for a in range(reach):
                        if 0 <= d + a < tiles:
                            sums[d + a] = sums[d + a] + factor[a] * value
                return tuple(sums)

            zero = jnp.zeros((SUB, LANES), jnp.float32)
            sums = lax.fori_loop(0, SUB, phase, (zero,) * tiles)
            filtered = jnp.concatenate(sums, axis=0)
            cols = pl.ds(n * LANES, LANES)
            a_buf[z, pl.ds(base, ROWS), cols] = (
                q_v[pl.ds(base, ROWS), cols].astype(jnp.float32) * filtered
            ).astype(jnp.bfloat16)

    loads[3].wait()
    loads[4].wait()
    for n in range(width // LANES):
        flat = t_v[n * LANES : (n + 1) * LANES, :].T
        taps[n] = jnp.broadcast_to(flat[:, None, :], taps.shape[1:])
        taps[n, 0] = taps[n, 0] + g_v[:, n * LANES : (n + 1) * LANES]

    loads[5].wait()
    filter_chunk(0)

    def a_copy(i, way, hop):
        step = 1 if way == 0 else -1
        block = a_buf.at[(z + nz - step * hop) % nz, pl.ds(order[i] * ROWS, ROWS), :]
        return pltpu.make_async_remote_copy(
            src_ref=block,
            dst_ref=block,
            send_sem=a_send_sem,
            recv_sem=a_recv_sem.at[i, way, hop],
            device_id=z_up if way == 0 else z_down,
            device_id_type=MESH,
        )

    def a_arrived(i, way, hop):
        step = 1 if way == 0 else -1
        block = a_buf.at[
            (z + nz - step * (hop + 1)) % nz, pl.ds(order[i] * ROWS, ROWS), :
        ]
        pltpu.make_async_copy(block, block, a_recv_sem.at[i, way, hop]).wait()

    def a_forward(i, way, hop):
        a_arrived(i, way, hop)
        if hop + 1 < hops(nz, i % 2 == 0)[way]:
            a_copy(i, way, hop + 1).start()

    def piece_column(p):
        return (x + (2, 1, 3, 0)[p]) % X

    def b_block(p, owner, core):
        rows = pl.ds(pl.multiple_of((2 * owner + core) * half, half), half)
        return b_buf.at[piece_column(p), rows, :]

    def b_copy(p, way, hop):
        step = 1 if way == 0 else -1
        block = b_block(p, (y + ny - step * hop) % ny, c)
        return pltpu.make_async_remote_copy(
            src_ref=block,
            dst_ref=block,
            send_sem=b_send_sem,
            recv_sem=b_recv_sem.at[p, way, hop],
            device_id=y_up if way == 0 else y_down,
            device_id_type=MESH,
        )

    def to_sibling(p, owner):
        block = b_block(p, owner, c)
        pltpu.make_async_remote_copy(
            src_ref=block,
            dst_ref=block,
            send_sem=m_send_sem,
            recv_sem=m_recv_sem.at[p, owner],
            device_id=sibling,
            device_id_type=MESH,
        ).start()

    def b_start(p):
        column = piece_column(p)
        block = b_block(p, y, c)
        pltpu.make_async_copy(block, block, t_recv_sem.at[column]).wait()
        for way in range(2):
            if hops(ny, p % 2 == 0)[way]:
                b_copy(p, way, 0).start()
        to_sibling(p, y)

    def b_forward(p, way, hop):
        step = 1 if way == 0 else -1
        owner = (y + ny - step * (hop + 1)) % ny
        block = b_block(p, owner, c)
        pltpu.make_async_copy(block, block, b_recv_sem.at[p, way, hop]).wait()
        if hop + 1 < hops(ny, p % 2 == 0)[way]:
            b_copy(p, way, hop + 1).start()
        to_sibling(p, owner)

    def b_whole(p):
        for owner in range(ny):
            block = b_block(p, owner, 1 - c)
            pltpu.make_async_copy(block, block, m_recv_sem.at[p, owner]).wait()

    def multiply(i, p):
        rows = pl.ds(order[i] * ROWS, ROWS)
        left = jnp.concatenate([a_buf[k, rows, :] for k in range(nz)], axis=1)
        total = jnp.dot(
            left, b_buf[piece_column(p)], preferred_element_type=jnp.float32
        )
        if p == X - 1:
            own[rows, :] = total
            return
        c_send[p, rows, :] = total.astype(jnp.bfloat16)
        pltpu.make_async_remote_copy(
            src_ref=c_send.at[p, rows, :],
            dst_ref=c_recv.at[p, rows, :],
            send_sem=c_send_sem,
            recv_sem=c_recv_sem.at[i, p],
            device_id=at(y, c, z, piece_column(p)),
            device_id_type=MESH,
        ).start()

    def finish(i):
        rows = pl.ds(order[i] * ROWS, ROWS)
        total = own[rows, :]
        for p in range(X - 1):
            block = c_recv.at[p, rows, :]
            pltpu.make_async_copy(block, block, c_recv_sem.at[i, p]).wait()
            total = total + c_recv[p, rows, :].astype(jnp.float32)
        o_ref[rows, :] = total.astype(jnp.bfloat16)

    def a_begin(i):
        for way in range(2):
            if hops(nz, i % 2 == 0)[way]:
                a_copy(i, way, 0).start()

    work = {
        FILTER: filter_chunk,
        A_BEGIN: a_begin,
        A_FORWARD: a_forward,
        B_BEGIN: b_start,
        B_FORWARD: b_forward,
        B_WHOLE: b_whole,
        MULTIPLY: multiply,
        FINISH: finish,
    }
    for name, *where in PLAN:
        work[name](*where)

    for here, remote, local in turns:
        pl.when(jnp.logical_not(here))(remote.wait_send)
    halo.wait_send()
    sent = a_buf.at[pl.ds(0, nz - 1)]
    pltpu.make_async_copy(sent, sent, a_send_sem).wait()
    sent = b_buf.at[:, pl.ds(0, (ny - 1) * half), :]
    pltpu.make_async_copy(sent, sent, b_send_sem).wait()
    sent = b_buf.at[:, pl.ds(0, ny * half), :]
    pltpu.make_async_copy(sent, sent, m_send_sem).wait()
    pltpu.make_async_copy(c_send, c_send, c_send_sem).wait()


def on_device(ny, nz, q, k, v, earlier, taps, gain, weight, scales):
    tokens, width = q.shape
    depth = weight.shape[0]
    reach = taps.shape[1]
    chunks = tokens // ROWS
    vmem, dma = pltpu.VMEM, pltpu.SemaphoreType.DMA
    bf16, f32 = jnp.bfloat16, jnp.float32
    anywhere = pl.BlockSpec(memory_space=pltpu.HBM)
    gain = gain.reshape(1, width)
    return pl.pallas_call(
        functools.partial(kernel, ny, nz),
        out_shape=pltpu.VMEM((tokens, width), bf16),
        in_specs=[anywhere] * 7 + [pl.BlockSpec(memory_space=pltpu.SMEM)],
        out_specs=pl.BlockSpec(memory_space=pltpu.VMEM),
        scratch_shapes=[
            vmem(q.shape, bf16),
            vmem(k.shape, bf16),
            vmem(v.shape, bf16),
            vmem(earlier.shape, bf16),
            vmem(taps.shape, f32),
            vmem(gain.shape, f32),
            vmem(weight.shape, bf16),
            vmem((ROWS, width), bf16),
            vmem((ROWS, width), bf16),
            vmem((width // LANES, ROWS + tokens, LANES), f32),
            vmem((width // LANES, reach, SUB, LANES), f32),
            vmem((depth, width), bf16),
            vmem((nz, tokens, width), bf16),
            vmem((X, nz * width, width), bf16),
            vmem((X - 1, tokens, width), bf16),
            vmem((X - 1, tokens, width), bf16),
            vmem((tokens, width), f32),
            dma((7,)),
            dma((2,)),
            dma,
            dma((chunks, 2, nz // 2)),
            dma,
            dma((X, 2, ny // 2)),
            dma,
            dma((X, ny)),
            dma((2, CORES)),
            dma((X,)),
            dma,
            dma((chunks, X - 1)),
        ],
        compiler_params=pltpu.CompilerParams(
            collective_id=0, has_side_effects=True, vmem_limit_bytes=63 * 1024 * 1024
        ),
        cost_estimate=pl.CostEstimate(
            flops=2 * tokens * nz * width * X * width,
            bytes_accessed=4 * tokens * width * 2,
            transcendentals=0,
        ),
    )(q, k, v, earlier, taps, gain, weight, scales.T)


def solution(mesh):
    ny = mesh.shape["seq"] // CORES
    nz = mesh.shape["hid"] // X
    return jax.shard_map(
        functools.partial(on_device, ny, nz),
        mesh=mesh,
        in_specs=(
            P("seq", "hid"),
            P("seq", "hid"),
            P("seq", "hid"),
            P(None, "hid"),
            P("hid", None),
            P("hid"),
            P("seq", "hid"),
            P("seq", "hid"),
        ),
        out_specs=P("seq", "hid"),
        check_vma=False,
    )
```

```python
import functools

import jax
import jax.numpy as jnp
from jax import lax
from jax.experimental import pallas as pl
from jax.experimental.pallas import tpu as pltpu
from jax.sharding import PartitionSpec as P

MESH = pl.DeviceIdType.MESH
X = 4
CORES = 2
BLOCK = 128
LANES = 128
SUB = 8
ROWS = 128
FILTER, A_BEGIN, A_FORWARD, B_BEGIN, B_FORWARD, B_WHOLE, MULTIPLY, FINISH = range(8)
PLAN = (
    (A_BEGIN, 0), (FILTER, 1), (B_BEGIN, 0), (A_BEGIN, 1), (FILTER, 2), (B_BEGIN, 1), (A_BEGIN, 2), (FILTER, 3),
    (A_FORWARD, 0, 0, 0), (A_FORWARD, 0, 1, 0), (B_BEGIN, 2), (B_FORWARD, 0, 0, 0), (A_FORWARD, 1, 0, 0),
    (A_FORWARD, 1, 1, 0), (B_FORWARD, 0, 1, 0), (FILTER, 4), (B_FORWARD, 1, 0, 0), (A_FORWARD, 2, 0, 0),
    (A_FORWARD, 2, 1, 0), (B_FORWARD, 1, 1, 0), (FILTER, 5), (A_FORWARD, 0, 0, 1), (A_FORWARD, 0, 1, 1),
    (B_FORWARD, 2, 0, 0), (B_FORWARD, 2, 1, 0), (A_FORWARD, 1, 0, 1), (A_FORWARD, 1, 1, 1), (B_FORWARD, 0, 0, 1),
    (B_FORWARD, 0, 1, 1), (A_FORWARD, 2, 0, 1), (A_FORWARD, 2, 1, 1), (B_FORWARD, 1, 0, 1), (B_FORWARD, 1, 1, 1),
    (A_FORWARD, 0, 0, 2), (A_FORWARD, 0, 1, 2), (B_FORWARD, 2, 0, 1), (B_FORWARD, 2, 1, 1), (A_BEGIN, 3),
    (A_FORWARD, 1, 0, 2), (A_FORWARD, 1, 1, 2), (B_FORWARD, 0, 0, 2), (B_FORWARD, 0, 1, 2), (B_BEGIN, 3),
    (B_FORWARD, 1, 0, 2), (A_FORWARD, 2, 0, 2), (B_FORWARD, 1, 1, 2), (A_FORWARD, 2, 1, 2), (A_BEGIN, 4),
    (A_FORWARD, 0, 0, 3), (A_FORWARD, 3, 1, 0), (B_FORWARD, 2, 0, 2), (B_FORWARD, 2, 1, 2), (A_FORWARD, 1, 1, 3),
    (A_FORWARD, 3, 0, 0), (B_FORWARD, 0, 0, 3), (B_FORWARD, 3, 1, 0), (A_BEGIN, 5), (A_FORWARD, 2, 0, 3),
    (A_FORWARD, 4, 1, 0), (B_FORWARD, 1, 1, 3), (B_FORWARD, 2, 0, 3), (B_FORWARD, 3, 0, 0), (B_WHOLE, 0),
    (MULTIPLY, 0, 0), (A_FORWARD, 3, 1, 1), (A_FORWARD, 4, 0, 0), (MULTIPLY, 1, 0), (MULTIPLY, 2, 0),
    (B_FORWARD, 3, 1, 1), (B_WHOLE, 1), (MULTIPLY, 0, 1), (A_FORWARD, 3, 0, 1), (A_FORWARD, 5, 1, 0),
    (MULTIPLY, 1, 1), (MULTIPLY, 2, 1), (B_FORWARD, 3, 0, 1), (B_WHOLE, 2), (MULTIPLY, 0, 2), (A_FORWARD, 4, 1, 1),
    (A_FORWARD, 5, 0, 0), (MULTIPLY, 1, 2), (MULTIPLY, 2, 2), (A_FORWARD, 3, 1, 2), (A_FORWARD, 4, 0, 1),
    (B_FORWARD, 3, 1, 2), (B_FORWARD, 3, 0, 2), (A_FORWARD, 3, 0, 2), (A_FORWARD, 5, 1, 1), (A_FORWARD, 4, 1, 2),
    (A_FORWARD, 5, 0, 1), (B_FORWARD, 3, 1, 3), (A_FORWARD, 3, 1, 3), (A_FORWARD, 4, 0, 2), (MULTIPLY, 3, 0),
    (MULTIPLY, 3, 1), (MULTIPLY, 3, 2), (A_FORWARD, 5, 1, 2), (B_WHOLE, 3), (MULTIPLY, 0, 3), (A_FORWARD, 5, 0, 2),
    (MULTIPLY, 1, 3), (MULTIPLY, 2, 3), (MULTIPLY, 3, 3), (A_FORWARD, 5, 1, 3), (FINISH, 0), (A_FORWARD, 4, 0, 3),
    (MULTIPLY, 4, 0), (MULTIPLY, 4, 1), (MULTIPLY, 4, 2), (MULTIPLY, 4, 3), (MULTIPLY, 5, 0), (MULTIPLY, 5, 1),
    (MULTIPLY, 5, 2), (MULTIPLY, 5, 3), (FINISH, 1), (FINISH, 2), (FINISH, 3), (FINISH, 4), (FINISH, 5),
)


def hops(n, even):
    far = n // 2
    return (far, n - 1 - far) if even else (n - 1 - far, far)


def kernel(
    ny,
    nz,
    q_hbm,
    k_hbm,
    v_hbm,
    e_hbm,
    t_hbm,
    g_hbm,
    w_hbm,
    s_ref,
    o_ref,
    q_v,
    k_v,
    v_v,
    e_v,
    t_v,
    g_v,
    w_v,
    halo_out,
    halo_in,
    ext,
    taps,
    deq,
    a_buf,
    b_buf,
    c_send,
    c_recv,
    own,
    in_sem,
    halo_sem,
    a_send_sem,
    a_recv_sem,
    b_send_sem,
    b_recv_sem,
    m_send_sem,
    m_recv_sem,
    t_send_sem,
    t_recv_sem,
    c_send_sem,
    c_recv_sem,
):
    tokens, width = q_v.shape
    chunks = tokens // ROWS
    half = ROWS
    s, hid = lax.axis_index("seq"), lax.axis_index("hid")
    y, c = s // CORES, s % CORES
    z, x = hid // X, hid % X

    def at(y_, c_, z_, x_):
        return (y_ * CORES + c_, z_ * X + x_)

    z_up, z_down = at(y, c, (z + 1) % nz, x), at(y, c, (z + nz - 1) % nz, x)
    y_up, y_down = at((y + 1) % ny, c, z, x), at((y + ny - 1) % ny, c, z, x)
    sibling = at(y, 1 - c, z, x)
    seq_next = ((s + 1) % (ny * CORES), hid)

    barrier = pltpu.get_barrier_semaphore()
    partners = [z_up, z_down, y_up, y_down]
    partners += [
        at(y, (c + dc) % CORES, z, (x + dx) % X)
        for dc in range(CORES)
        for dx in range(X)
        if (dc, dx) != (0, 0)
    ]
    partners += [at((y + ny + 2 * c - 1) % ny, 1 - c, z, x)]
    for partner in partners:
        pl.semaphore_signal(barrier, inc=1, device_id=partner, device_id_type=MESH)

    loads = [
        pltpu.make_async_copy(src, dst, in_sem.at[n])
        for n, (src, dst) in enumerate(
            (
                (w_hbm, w_v),
                (k_hbm, k_v),
                (v_hbm, v_v),
                (t_hbm, t_v),
                (g_hbm, g_v),
                (q_hbm, q_v),
                (e_hbm, e_v),
            )
        )
    ]
    for load in loads:
        load.start()

    loads[0].wait()
    for i in range(w_v.shape[0] // BLOCK):
        for n in range(width // BLOCK):
            rows, cols = pl.ds(i * BLOCK, BLOCK), pl.ds(n * BLOCK, BLOCK)
            deq[rows, cols] = (
                w_v[rows, cols].astype(jnp.float32) * s_ref[n, i]
            ).astype(jnp.bfloat16)

    def turn(e, core):
        here = (x == 2 * c + e) & (c == core)
        src = deq.at[pl.ds((2 * e + core) * half, half), :]
        dst = b_buf.at[x, pl.ds(pl.multiple_of((2 * y + core) * half, half), half), :]
        remote = pltpu.make_async_remote_copy(
            src_ref=src,
            dst_ref=dst,
            send_sem=t_send_sem.at[e, core],
            recv_sem=t_recv_sem.at[x],
            device_id=at(y, core, z, 2 * c + e),
            device_id_type=MESH,
        )
        local = pltpu.make_async_copy(src, dst, t_recv_sem.at[x])
        return here, remote, local

    turns = [turn(e, core) for e in range(2) for core in range(CORES)]
    pl.semaphore_wait(barrier, len(partners))
    for here, remote, local in turns:
        pl.when(jnp.logical_not(here))(remote.start)
        pl.when(here)(local.start)

    loads[1].wait()
    loads[2].wait()
    for i in range(chunks):
        rows = pl.ds(i * ROWS, ROWS)
        product = (
            k_v[rows, :].astype(jnp.float32) * v_v[rows, :].astype(jnp.float32)
        ).astype(jnp.bfloat16)
        if i == chunks - 1:
            halo_out[...] = product
        wide = product.astype(jnp.float32)
        for n in range(width // LANES):
            ext[n, pl.ds(ROWS + i * ROWS, ROWS), :] = wide[:, n * LANES : (n + 1) * LANES]

    halo = pltpu.make_async_remote_copy(
        src_ref=halo_out,
        dst_ref=halo_in,
        send_sem=halo_sem.at[0],
        recv_sem=halo_sem.at[1],
        device_id=seq_next,
        device_id_type=MESH,
    )
    halo.start()

    order = [(i + 1) % chunks for i in range(chunks)]

    def preceding():
        loads[6].wait()
        halo.wait_recv()

        @pl.when(s == 0)
        def _():
            early = e_v[...].astype(jnp.float32)
            for n in range(width // LANES):
                ext[n, pl.ds(1, ROWS - 1), :] = early[:, n * LANES : (n + 1) * LANES]

        @pl.when(s != 0)
        def _():
            early = halo_in[...].astype(jnp.float32)
            for n in range(width // LANES):
                ext[n, pl.ds(0, ROWS), :] = early[:, n * LANES : (n + 1) * LANES]

    def filter_chunk(i):
        base = order[i] * ROWS
        if base == 0:
            preceding()
        tiles = ROWS // SUB
        reach = taps.shape[1] // SUB
        for n in range(width // LANES):

            def phase(b, sums):
                sums = list(sums)
                factor = [taps[n, a * SUB + b] for a in range(reach)]
                for d in range(1 - reach, tiles):
                    value = ext[n, pl.ds(ROWS + base + d * SUB - b, SUB), :]
                    for a in range(reach):
                        if 0 <= d + a < tiles:
                            sums[d + a] = sums[d + a] + factor[a] * value
                return tuple(sums)

            zero = jnp.zeros((SUB, LANES), jnp.float32)
            sums = lax.fori_loop(0, SUB, phase, (zero,) * tiles)
            filtered = jnp.concatenate(sums, axis=0)
            cols = pl.ds(n * LANES, LANES)
            a_buf[z, pl.ds(base, ROWS), cols] = (
                q_v[pl.ds(base, ROWS), cols].astype(jnp.float32) * filtered
            ).astype(jnp.bfloat16)

    loads[3].wait()
    loads[4].wait()
    for n in range(width // LANES):
        flat = t_v[n * LANES : (n + 1) * LANES, :].T
        taps[n] = jnp.broadcast_to(flat[:, None, :], taps.shape[1:])
        taps[n, 0] = taps[n, 0] + g_v[:, n * LANES : (n + 1) * LANES]

    loads[5].wait()
    filter_chunk(0)

    def a_copy(i, way, hop):
        step = 1 if way == 0 else -1
        block = a_buf.at[(z + nz - step * hop) % nz, pl.ds(order[i] * ROWS, ROWS), :]
        return pltpu.make_async_remote_copy(
            src_ref=block,
            dst_ref=block,
            send_sem=a_send_sem,
            recv_sem=a_recv_sem.at[i, way, hop],
            device_id=z_up if way == 0 else z_down,
            device_id_type=MESH,
        )

    def a_arrived(i, way, hop):
        step = 1 if way == 0 else -1
        block = a_buf.at[
            (z + nz - step * (hop + 1)) % nz, pl.ds(order[i] * ROWS, ROWS), :
        ]
        pltpu.make_async_copy(block, block, a_recv_sem.at[i, way, hop]).wait()

    def a_forward(i, way, hop):
        a_arrived(i, way, hop)
        if hop + 1 < hops(nz, i % 2 == 0)[way]:
            a_copy(i, way, hop + 1).start()

    def piece_column(p):
        return (x + (2, 1, 3, 0)[p]) % X

    def b_block(p, owner, core):
        rows = pl.ds(pl.multiple_of((2 * owner + core) * half, half), half)
        return b_buf.at[piece_column(p), rows, :]

    def b_copy(p, way, hop):
        step = 1 if way == 0 else -1
        block = b_block(p, (y + ny - step * hop) % ny, c)
        return pltpu.make_async_remote_copy(
            src_ref=block,
            dst_ref=block,
            send_sem=b_send_sem,
            recv_sem=b_recv_sem.at[p, way, hop],
            device_id=y_up if way == 0 else y_down,
            device_id_type=MESH,
        )

    def to_sibling(p, owner):
        block = b_block(p, owner, c)
        pltpu.make_async_remote_copy(
            src_ref=block,
            dst_ref=block,
            send_sem=m_send_sem,
            recv_sem=m_recv_sem.at[p],
            device_id=sibling,
            device_id_type=MESH,
        ).start()

    def b_start(p):
        column = piece_column(p)
        block = b_block(p, y, c)
        pltpu.make_async_copy(block, block, t_recv_sem.at[column]).wait()
        for way in range(2):
            if hops(ny, p % 2 == 0)[way]:
                b_copy(p, way, 0).start()
        to_sibling(p, y)

    def b_forward(p, way, hop):
        step = 1 if way == 0 else -1
        owner = (y + ny - step * (hop + 1)) % ny
        block = b_block(p, owner, c)
        pltpu.make_async_copy(block, block, b_recv_sem.at[p, way, hop]).wait()
        if hop + 1 < hops(ny, p % 2 == 0)[way]:
            b_copy(p, way, hop + 1).start()
        to_sibling(p, owner)

    def b_whole(p):
        blocks = b_buf.at[piece_column(p), pl.ds(0, ny * half), :]
        pltpu.make_async_copy(blocks, blocks, m_recv_sem.at[p]).wait()

    def multiply(i, p):
        rows = pl.ds(order[i] * ROWS, ROWS)
        left = jnp.concatenate([a_buf[k, rows, :] for k in range(nz)], axis=1)
        total = jnp.dot(
            left, b_buf[piece_column(p)], preferred_element_type=jnp.float32
        )
        if p == X - 1:
            own[rows, :] = total
            return
        c_send[p, rows, :] = total.astype(jnp.bfloat16)
        pltpu.make_async_remote_copy(
            src_ref=c_send.at[p, rows, :],
            dst_ref=c_recv.at[p, rows, :],
            send_sem=c_send_sem,
            recv_sem=c_recv_sem.at[i, p],
            device_id=at(y, c, z, piece_column(p)),
            device_id_type=MESH,
        ).start()

    def finish(i):
        rows = pl.ds(order[i] * ROWS, ROWS)
        total = own[rows, :]
        for p in range(X - 1):
            block = c_recv.at[p, rows, :]
            pltpu.make_async_copy(block, block, c_recv_sem.at[i, p]).wait()
            total = total + c_recv[p, rows, :].astype(jnp.float32)
        o_ref[rows, :] = total.astype(jnp.bfloat16)

    def a_begin(i):
        for way in range(2):
            if hops(nz, i % 2 == 0)[way]:
                a_copy(i, way, 0).start()

    work = {
        FILTER: filter_chunk,
        A_BEGIN: a_begin,
        A_FORWARD: a_forward,
        B_BEGIN: b_start,
        B_FORWARD: b_forward,
        B_WHOLE: b_whole,
        MULTIPLY: multiply,
        FINISH: finish,
    }
    for name, *where in PLAN:
        work[name](*where)

    for here, remote, local in turns:
        pl.when(jnp.logical_not(here))(remote.wait_send)
    halo.wait_send()
    sent = a_buf.at[pl.ds(0, nz - 1)]
    pltpu.make_async_copy(sent, sent, a_send_sem).wait()
    sent = b_buf.at[:, pl.ds(0, (ny - 1) * half), :]
    pltpu.make_async_copy(sent, sent, b_send_sem).wait()
    sent = b_buf.at[:, pl.ds(0, ny * half), :]
    pltpu.make_async_copy(sent, sent, m_send_sem).wait()
    pltpu.make_async_copy(c_send, c_send, c_send_sem).wait()


def on_device(ny, nz, q, k, v, earlier, taps, gain, weight, scales):
    tokens, width = q.shape
    depth = weight.shape[0]
    reach = taps.shape[1]
    chunks = tokens // ROWS
    vmem, dma = pltpu.VMEM, pltpu.SemaphoreType.DMA
    bf16, f32 = jnp.bfloat16, jnp.float32
    anywhere = pl.BlockSpec(memory_space=pltpu.HBM)
    gain = gain.reshape(1, width)
    return pl.pallas_call(
        functools.partial(kernel, ny, nz),
        out_shape=pltpu.VMEM((tokens, width), bf16),
        in_specs=[anywhere] * 7 + [pl.BlockSpec(memory_space=pltpu.SMEM)],
        out_specs=pl.BlockSpec(memory_space=pltpu.VMEM),
        scratch_shapes=[
            vmem(q.shape, bf16),
            vmem(k.shape, bf16),
            vmem(v.shape, bf16),
            vmem(earlier.shape, bf16),
            vmem(taps.shape, f32),
            vmem(gain.shape, f32),
            vmem(weight.shape, bf16),
            vmem((ROWS, width), bf16),
            vmem((ROWS, width), bf16),
            vmem((width // LANES, ROWS + tokens, LANES), f32),
            vmem((width // LANES, reach, SUB, LANES), f32),
            vmem((depth, width), bf16),
            vmem((nz, tokens, width), bf16),
            vmem((X, nz * width, width), bf16),
            vmem((X - 1, tokens, width), bf16),
            vmem((X - 1, tokens, width), bf16),
            vmem((tokens, width), f32),
            dma((7,)),
            dma((2,)),
            dma,
            dma((chunks, 2, nz // 2)),
            dma,
            dma((X, 2, ny // 2)),
            dma,
            dma((X,)),
            dma((2, CORES)),
            dma((X,)),
            dma,
            dma((chunks, X - 1)),
        ],
        compiler_params=pltpu.CompilerParams(
            collective_id=0, has_side_effects=True, vmem_limit_bytes=63 * 1024 * 1024
        ),
        cost_estimate=pl.CostEstimate(
            flops=2 * tokens * nz * width * X * width,
            bytes_accessed=4 * tokens * width * 2,
            transcendentals=0,
        ),
    )(q, k, v, earlier, taps, gain, weight, scales.T)


def solution(mesh):
    ny = mesh.shape["seq"] // CORES
    nz = mesh.shape["hid"] // X
    return jax.shard_map(
        functools.partial(on_device, ny, nz),
        mesh=mesh,
        in_specs=(
            P("seq", "hid"),
            P("seq", "hid"),
            P("seq", "hid"),
            P(None, "hid"),
            P("hid", None),
            P("hid"),
            P("seq", "hid"),
            P("seq", "hid"),
        ),
        out_specs=P("seq", "hid"),
        check_vma=False,
    )
```
